32 devices in a mesh: gx: 8 (over z, y), gy: 4 (over x, core).
Axes of the slice: x: 2, y: 2, z: 4, core: 2. Of those that a mesh axis runs over, the one named last changes fastest.
Arguments:
- features: float32 [8192, 1024], P(('gx', 'gy')), may hold values from -6 to 6
- labels: int32 [32], replicated, may hold values from 0 to 1, as said below
- rounds: int32 [2], replicated, may hold values from 1 to 31, as said below
Outputs:
- feature_grad: float32 [8192, 1024], P(('gx', 'gy'))
The draws below stay inside these ranges and needn't reach their ends.
Inputs may be any that keep to these rules, and one draw needn't show every extreme that they name: Each of the two values labels some block. `rounds`: 2 different nonzero masks, one of which flips every bit of the block index.
All inputs are finite; a program needn't handle non-finite values.
Results may differ from the reference program's by a relative error of at most 0.0003.
Values sent between devices are 32-bit elements; how exact they have to be, the bound alone decides.
A program may use at most 64 MiB of HBM per device.

```python
import jax
import jax.numpy as jnp
from jax import lax

D = 1024
ROWS_DEV = 256
ROUNDS = 2
BLOCKS = 32
ROWS_ALL = 8192


def draw_labels(key, part):
    key = jax.random.fold_in(key, 11)
    key_bits, key_order = jax.random.split(key)
    values = jax.random.randint(key_bits, (BLOCKS,), 0, 2).astype(jnp.int32)
    placing = jax.random.permutation(key_order, BLOCKS)
    values = values.at[placing[0]].set(1)
    values = values.at[placing[1]].set(0)
    return values.astype(jnp.int32)


def draw_rounds(key, part):
    key = jax.random.fold_in(key, 23)
    key_pick, key_place = jax.random.split(key)
    others = jax.random.permutation(key_pick, BLOCKS - 2)[:ROUNDS - 1] + 1
    full_flip = jnp.full((1,), BLOCKS - 1, dtype=jnp.int32)
    joined = jnp.concatenate([others.astype(jnp.int32), full_flip])
    placed = jax.random.permutation(key_place, joined)
    return placed.astype(jnp.int32)


def steps_of(stream_key, extent, cuts, low, top_value):
    def one(axis_at, parts):
        steps = jax.random.uniform(jax.random.fold_in(jax.random.fold_in(stream_key, 6), axis_at), (parts,), jnp.float32, low / len(cuts), top_value / len(cuts))
        return jnp.repeat(jnp.exp(steps), extent[axis_at] // parts).reshape((-1,) + (1,) * (len(extent) - axis_at - 1))

    gain = one(*cuts[0])
    for cut in cuts[1:]:
        gain = gain * one(*cut)
    return gain


def normal_values(stream_key, dims, scale, limit, cuts=(), kind=jnp.bfloat16):
    entries = scale * jax.random.normal(stream_key, dims, jnp.float32)
    if cuts:
        entries = entries * steps_of(stream_key, dims, cuts, -0.22, 0.18)
    return jnp.clip(entries, -limit, limit).astype(kind)


def setup_inputs(seed: int = 0) -> dict:
    arg_keys = jax.random.split(jax.random.key(seed), 4)
    return {
        "features": normal_values(arg_keys[0], (ROWS_ALL, D), 1.0, 6.0, ((0, 32),), jnp.float32),
        "labels": draw_labels(jax.random.fold_in(arg_keys[3], 71), 0),
        "rounds": draw_rounds(jax.random.fold_in(arg_keys[3], 71), 0),
    }


def pair_weight(label_own, label_other, real_rows, fake_rows, loss_scale):
    both_real = loss_scale / (real_rows * (real_rows - 1.0))
    both_fake = loss_scale / (fake_rows * (fake_rows - 1.0))
    mixed = -loss_scale / (real_rows * fake_rows)
    same = label_own == label_other
    return jnp.where(same, jnp.where(label_own == 1, both_real, both_fake), mixed)

def tile_grad(own_rows, partner, weight, skip_diag):
    root_width = jnp.sqrt(jnp.float32(D))
    scores = jnp.dot(own_rows, partner.T, precision=lax.Precision.HIGHEST) / root_width
    coefficient = weight * (6.0 / root_width) * (scores + 1.0) ** 2
    if skip_diag:
        coefficient = jnp.where(jnp.eye(ROWS_DEV, dtype=bool), jnp.float32(0.0), coefficient)
    return jnp.dot(coefficient, partner, precision=lax.Precision.HIGHEST)

def reference(features, labels, rounds):
    real_rows = jnp.float32(ROWS_DEV) * jnp.sum(labels).astype(jnp.float32)
    fake_rows = jnp.float32(ROWS_ALL) - real_rows
    loss_scale = float(ROWS_ALL) * float(ROWS_ALL) / 16.0

    def one_block(block_id):
        own_rows = lax.dynamic_slice_in_dim(features, (block_id * ROWS_DEV).astype(jnp.int32), ROWS_DEV, 0)
        label_own = labels[block_id]
        gradient = tile_grad(own_rows, own_rows, pair_weight(label_own, label_own, real_rows, fake_rows, loss_scale), True)
        for round_index in range(ROUNDS):
            partner_id = jnp.bitwise_xor(block_id, rounds[round_index]).astype(jnp.int32)
            partner = lax.dynamic_slice_in_dim(features, (partner_id * ROWS_DEV).astype(jnp.int32), ROWS_DEV, 0)
            weight = pair_weight(label_own, labels[partner_id], real_rows, fake_rows, loss_scale)
            gradient = gradient + tile_grad(own_rows, partner, weight, False)
        return gradient
    gradients = lax.map(one_block, jnp.arange(BLOCKS, dtype=jnp.int32))
    return gradients.reshape(ROWS_ALL, D)
```

```python
import functools

import jax
import jax.numpy as jnp
from jax import lax
from jax.experimental import pallas as pl
from jax.experimental.pallas import tpu as pltpu
from jax.sharding import PartitionSpec as P

MESH = pl.DeviceIdType.MESH
CHUNKS = 8
GROUPS = 2
KERNEL_DEVICES = 64


def pair_weight(label_own, label_other, real_rows, fake_rows, loss_scale):
    both_real = loss_scale / (real_rows * (real_rows - 1.0))
    both_fake = loss_scale / (fake_rows * (fake_rows - 1.0))
    mixed = -loss_scale / (real_rows * fake_rows)
    same = label_own == label_other
    return jnp.where(same, jnp.where(label_own == 1, both_real, both_fake), mixed)


def flipped(index, mask):
    result = index
    bit = 1
    while bit <= mask:
        if mask & bit:
            result = result + bit * (1 - 2 * ((index // bit) % 2))
        bit *= 2
    return result


def split(values):
    high = values.astype(jnp.bfloat16)
    low = (values - high.astype(jnp.float32)).astype(jnp.bfloat16)
    return high, low


def dot_t(left, right):
    return lax.dot_general(
        left, right, (((1,), (1,)), ((), ())), preferred_element_type=jnp.float32
    )


def dot(left, right):
    return jnp.dot(left, right, preferred_element_type=jnp.float32)


def exchange_kernel(
    mask, across, down, labels_ref, block_ref, grad_ref, held, own_high, own_low,
    load_sem, send_near, recv_near, send_far, recv_far,
):
    rows, width = block_ref.shape
    blocks = across * down
    chunk = rows // CHUNKS
    group = rows // GROUPS
    own = lax.axis_index("gx") * down + lax.axis_index("gy")
    near = flipped(own, mask)
    far = flipped(own, (blocks - 1) ^ mask)
    flip = flipped(own, blocks - 1)

    def device(index):
        return (index // down, index % down)

    load = pltpu.make_async_copy(block_ref, held.at[pl.ds(0, rows)], load_sem)
    load.start()

    barrier = pltpu.get_barrier_semaphore()
    for peer in (near, far):
        pl.semaphore_signal(barrier, inc=1, device_id=device(peer), device_id_type=MESH)
    pl.semaphore_wait(barrier, 2)

    def to_near(at):
        return pltpu.make_async_remote_copy(
            src_ref=block_ref.at[pl.ds(at * chunk, chunk)],
            dst_ref=held.at[pl.ds(rows + at * chunk, chunk)],
            send_sem=send_near.at[at],
            recv_sem=recv_near.at[at],
            device_id=device(near),
            device_id_type=MESH,
        )

    def to_far(at):
        return pltpu.make_async_remote_copy(
            src_ref=held.at[pl.ds(rows + at * chunk, chunk)],
            dst_ref=held.at[pl.ds(2 * rows + at * chunk, chunk)],
            send_sem=send_far.at[at],
            recv_sem=recv_far.at[at],
            device_id=device(far),
            device_id_type=MESH,
        )

    def each(first, count, body):
        def step(at, carry):
            body(first + at)
            return carry

        lax.fori_loop(0, count, step, 0)

    each(0, CHUNKS, lambda at: to_near(at).start())

    label_sum = lax.fori_loop(
        0, blocks, lambda at, total: total + labels_ref[at], jnp.int32(0)
    )
    all_rows = rows * blocks
    real_rows = (label_sum * rows).astype(jnp.float32)
    fake_rows = jnp.float32(all_rows) - real_rows
    loss_scale = float(all_rows) * float(all_rows) / 16.0
    label_own = labels_ref[own]
    root_width = float(width) ** 0.5
    weights = [
        pair_weight(label_own, label, real_rows, fake_rows, loss_scale) * (6.0 / root_width)
        for label in (label_own, labels_ref[near], labels_ref[flip])
    ]

    load.wait()

    def prepare(at):
        here = pl.ds(at * chunk, chunk)
        high, low = split(held[here, :])
        own_high[here, :] = high
        own_low[here, :] = low
        grad_ref[here, :] = jnp.zeros((chunk, width), jnp.float32)

    each(0, CHUNKS, prepare)

    def relay(at):
        to_near(at).wait_recv()
        to_far(at).start()

    def tile(at, carry):
        which = at // GROUPS
        each(at + which * (2 * at - 4), (2 + 9 * which - 5 * which * which) // 2, relay)
        each(
            (CHUNKS // GROUPS) * (at % GROUPS),
            (CHUNKS // GROUPS) * (which // 2),
            lambda piece: to_far(piece).wait_recv(),
        )
        high, low = split(held[pl.ds(at * group, group), :])
        scores = (
            dot_t(own_high[...], high) + dot_t(own_high[...], low) + dot_t(own_low[...], high)
        ) * (1.0 / root_width)
        weight = jnp.where(which == 0, weights[0], jnp.where(which == 1, weights[1], weights[2]))
        raised = scores + 1.0
        coefficient = weight * (raised * raised)
        row = lax.broadcasted_iota(jnp.int32, (rows, group), 0)
        column = lax.broadcasted_iota(jnp.int32, (rows, group), 1) + at * group
        coefficient = jnp.where(row == column, 0.0, coefficient)
        c_high, c_low = split(coefficient)
        step = 256
        for start in range(0, width, step):
            here = slice(start, start + step)
            grad_ref[:, here] += (
                dot(c_high, high[:, here]) + dot(c_high, low[:, here]) + dot(c_low, high[:, here])
            )
        return carry

    lax.fori_loop(0, 3 * GROUPS, tile, 0)

    def finish(at):
        to_near(at).wait_send()
        to_far(at).wait_send()

    each(0, CHUNKS, finish)


def by_kernel(features, labels, mask, across, down):
    rows, width = features.shape
    blocks = across * down

    def branch(value):
        def call(features, labels):
            return pl.pallas_call(
                functools.partial(exchange_kernel, value, across, down),
                out_shape=jax.ShapeDtypeStruct((rows, width), jnp.float32),
                in_specs=[
                    pl.BlockSpec(memory_space=pltpu.SMEM),
                    pl.BlockSpec(memory_space=pl.ANY),
                ],
                out_specs=pl.BlockSpec(memory_space=pltpu.VMEM),
                scratch_shapes=[
                    pltpu.VMEM((3 * rows, width), jnp.float32),
                    pltpu.VMEM((rows, width), jnp.bfloat16),
                    pltpu.VMEM((rows, width), jnp.bfloat16),
                    pltpu.SemaphoreType.DMA,
                    pltpu.SemaphoreType.DMA((CHUNKS,)),
                    pltpu.SemaphoreType.DMA((CHUNKS,)),
                    pltpu.SemaphoreType.DMA((CHUNKS,)),
                    pltpu.SemaphoreType.DMA((CHUNKS,)),
                ],
                compiler_params=pltpu.CompilerParams(
                    collective_id=value,
                    has_side_effects=True,
                    vmem_limit_bytes=32 * 1024 * 1024,
                ),
                cost_estimate=pl.CostEstimate(
                    flops=36 * rows * rows * width,
                    bytes_accessed=12 * rows * width,
                    transcendentals=0,
                ),
                name="mmd_mask_%d" % value,
            )(labels, features)

        return call

    return lax.switch(
        mask - 1, [branch(value) for value in range(1, blocks - 1)], features, labels
    )


def tile_grad(own_rows, partner, weight, skip_diag):
    row_count, feat_width = own_rows.shape
    root_width = jnp.sqrt(jnp.float32(feat_width))
    scores = jnp.dot(own_rows, partner.T, precision=lax.Precision.HIGHEST) / root_width
    coefficient = weight * (6.0 / root_width) * (scores + 1.0) ** 2
    if skip_diag:
        coefficient = jnp.where(jnp.eye(row_count, dtype=bool), jnp.float32(0.0), coefficient)
    return jnp.dot(coefficient, partner, precision=lax.Precision.HIGHEST)


def permuted(values, axis, size, mask):
    def branch(value):
        pairs = [(at, at ^ value) for at in range(size)]
        return lambda values: lax.ppermute(values, axis, pairs)

    return lax.switch(mask, [branch(value) for value in range(size)], values)


def by_permutes(features, labels, mask, across, down):
    blocks = across * down
    own = lax.axis_index("gx") * down + lax.axis_index("gy")
    near = permuted(permuted(features, "gx", across, mask // down), "gy", down, mask % down)
    pairs = [(at, blocks - 1 - at) for at in range(blocks)]
    flip = lax.ppermute(features, ("gx", "gy"), pairs)
    all_rows = features.shape[0] * blocks
    real_rows = jnp.float32(features.shape[0]) * jnp.sum(labels).astype(jnp.float32)
    fake_rows = jnp.float32(all_rows) - real_rows
    loss_scale = float(all_rows) * float(all_rows) / 16.0

    def weight(other):
        return pair_weight(labels[own], labels[other], real_rows, fake_rows, loss_scale)

    return (
        tile_grad(features, features, weight(own), True)
        + tile_grad(features, near, weight(jnp.bitwise_xor(own, mask)), False)
        + tile_grad(features, flip, weight(blocks - 1 - own), False)
    )


def solution(mesh):
    across, down = mesh.shape["gx"], mesh.shape["gy"]
    blocks = across * down

    def on_device(features, labels, rounds):
        mask = jnp.bitwise_xor(jnp.bitwise_xor(rounds[0], rounds[1]), blocks - 1)
        form = by_kernel if blocks <= KERNEL_DEVICES else by_permutes
        return form(features, labels, mask, across, down)

    return jax.shard_map(
        on_device,
        mesh=mesh,
        in_specs=(P(("gx", "gy"), None), P(), P()),
        out_specs=P(("gx", "gy"), None),
        check_vma=False,
    )
```

```python
import functools

import jax
import jax.numpy as jnp
from jax import lax
from jax.experimental import pallas as pl
from jax.experimental.pallas import tpu as pltpu
from jax.sharding import PartitionSpec as P

MESH = pl.DeviceIdType.MESH
CHUNKS = 16
GROUPS = 4
WINDOW = 3
DIRECT = 2
KERNEL_DEVICES = 64


def pair_weight(label_own, label_other, real_rows, fake_rows, loss_scale):
    both_real = loss_scale / (real_rows * (real_rows - 1.0))
    both_fake = loss_scale / (fake_rows * (fake_rows - 1.0))
    mixed = -loss_scale / (real_rows * fake_rows)
    same = label_own == label_other
    return jnp.where(same, jnp.where(label_own == 1, both_real, both_fake), mixed)


def flipped(index, mask):
    result = index
    bit = 1
    while bit <= mask:
        if mask & bit:
            result = result + bit * (1 - 2 * ((index // bit) % 2))
        bit *= 2
    return result


def split(values):
    high = values.astype(jnp.bfloat16)
    low = (values - high.astype(jnp.float32)).astype(jnp.bfloat16)
    return high, low


def dot_t(left, right):
    return lax.dot_general(
        left, right, (((1,), (1,)), ((), ())), preferred_element_type=jnp.float32
    )


def dot(left, right):
    return jnp.dot(left, right, preferred_element_type=jnp.float32)


def pick_kernel(across, down, rows, width, rounds_ref, labels_ref, pick_ref, weights_ref):
    blocks = across * down
    own = lax.axis_index("gx") * down + lax.axis_index("gy")
    mask = jnp.bitwise_xor(jnp.bitwise_xor(rounds_ref[0], rounds_ref[1]), blocks - 1)
    pick_ref[0] = mask - 1
    label_sum = lax.fori_loop(
        0, blocks, lambda at, total: total + labels_ref[at], jnp.int32(0)
    )
    all_rows = rows * blocks
    real_rows = (label_sum * rows).astype(jnp.float32)
    fake_rows = jnp.float32(all_rows) - real_rows
    loss_scale = float(all_rows) * float(all_rows) / 16.0
    label_own = labels_ref[own]
    others = (label_own, labels_ref[jnp.bitwise_xor(own, mask)], labels_ref[blocks - 1 - own])
    for at, label in enumerate(others):
        weight = pair_weight(label_own, label, real_rows, fake_rows, loss_scale)
        weights_ref[at] = weight * (6.0 / float(width) ** 0.5)


def exchange_kernel(
    mask, across, down, weights_ref, block_ref, grad_ref, held, own_high, own_low,
    load_sem, send_near, recv_near, send_far, recv_far,
):
    rows, width = block_ref.shape
    blocks = across * down
    crossing = 2 * mask >= blocks
    direct = 0 if crossing else DIRECT
    chunk = rows // CHUNKS
    group = rows // GROUPS
    per_group = CHUNKS // GROUPS
    own = lax.axis_index("gx") * down + lax.axis_index("gy")
    near = flipped(own, mask)
    far = flipped(own, (blocks - 1) ^ mask)
    flip = flipped(own, blocks - 1)
    peers = (near, far, flip) if direct else (near, far)

    def device(index):
        return (index // down, index % down)

    load = pltpu.make_async_copy(block_ref, held.at[pl.ds(0, rows)], load_sem)
    load.start()

    barrier = pltpu.get_barrier_semaphore()
    for peer in peers:
        pl.semaphore_signal(barrier, inc=1, device_id=device(peer), device_id_type=MESH)
    pl.semaphore_wait(barrier, len(peers))

    def to_near(at):
        return pltpu.make_async_remote_copy(
            src_ref=block_ref.at[pl.ds(at * chunk, chunk)],
            dst_ref=held.at[pl.ds(rows + at * chunk, chunk)],
            send_sem=send_near.at[at],
            recv_sem=recv_near.at[at],
            device_id=device(near),
            device_id_type=MESH,
        )

    def to_far(at):
        return pltpu.make_async_remote_copy(
            src_ref=held.at[pl.ds(rows + at * chunk, chunk)],
            dst_ref=held.at[pl.ds(2 * rows + at * chunk, chunk)],
            send_sem=send_far.at[at],
            recv_sem=recv_far.at[at],
            device_id=device(far),
            device_id_type=MESH,
        )

    def to_flip(at):
        return pltpu.make_async_remote_copy(
            src_ref=block_ref.at[pl.ds(at * chunk, chunk)],
            dst_ref=held.at[pl.ds(2 * rows + at * chunk, chunk)],
            send_sem=send_far.at[at],
            recv_sem=recv_far.at[at],
            device_id=device(flip),
            device_id_type=MESH,
        )

    def each(first, count, body):
        def step(at, carry):
            body(first + at)
            return carry

        lax.fori_loop(0, count, step, 0)

    for at in range(direct):
        to_flip(at).start()
    each(0, WINDOW, lambda at: to_near(at).start())

    load.wait()

    def prepare(at):
        here = pl.ds(at * group, group)
        high, low = split(held[here, :])
        own_high[here, :] = high
        own_low[here, :] = low
        grad_ref[here, :] = jnp.zeros((group, width), jnp.float32)

    each(0, GROUPS, prepare)

    def relay(at):
        to_near(at).wait_recv()

        @pl.when(at >= direct)
        def _():
            to_far(at).start()

        to_near(at).wait_send()

        @pl.when(at + WINDOW < CHUNKS)
        def _():
            to_near(at + WINDOW).start()

    def tile(which, place):
        each(
            place * per_group, per_group * (which // 2), lambda at: to_far(at).wait_recv()
        )
        high, low = split(held[pl.ds(which * rows + place * group, group), :])
        scores = (
            dot_t(own_high[...], high) + dot_t(own_high[...], low) + dot_t(own_low[...], high)
        ) * (1.0 / float(width) ** 0.5)
        raised = scores + 1.0
        coefficient = weights_ref[which] * (raised * raised)
        row = lax.broadcasted_iota(jnp.int32, (rows, group), 0)
        column = lax.broadcasted_iota(jnp.int32, (rows, group), 1) + (which * rows + place * group)
        coefficient = jnp.where(row == column, 0.0, coefficient)
        c_high, c_low = split(coefficient)
        step = 256
        for start in range(0, width, step):
            here = slice(start, start + step)
            grad_ref[:, here] += (
                dot(c_high, high[:, here]) + dot(c_high, low[:, here]) + dot(c_low, high[:, here])
            )

    def advance(place):
        each(place * per_group, per_group, relay)
        if crossing:
            each(0, 2 + (place + GROUPS - 1) // GROUPS, lambda which: tile(which, place - which // 2))
        else:
            each(0, 2, lambda which: tile(which, place))

    each(0, GROUPS, advance)
    remaining = GROUPS - 1 if crossing else 0
    each(remaining, GROUPS - remaining, lambda place: tile(2, place))

    each(0, CHUNKS, lambda at: to_far(at).wait_send())


def by_kernel(features, labels, rounds, across, down):
    rows, width = features.shape
    blocks = across * down
    smem = pl.BlockSpec(memory_space=pltpu.SMEM)
    pick, weights = pl.pallas_call(
        functools.partial(pick_kernel, across, down, rows, width),
        out_shape=(
            jax.ShapeDtypeStruct((1,), jnp.int32),
            jax.ShapeDtypeStruct((3,), jnp.float32),
        ),
        in_specs=[smem, smem],
        out_specs=(smem, smem),
        compiler_params=pltpu.CompilerParams(vmem_limit_bytes=60 * 1024 * 1024),
        name="mmd_pick",
    )(rounds, labels)

    def branch(value):
        def call(features, weights):
            return pl.pallas_call(
                functools.partial(exchange_kernel, value, across, down),
                out_shape=jax.ShapeDtypeStruct((rows, width), jnp.float32),
                in_specs=[smem, pl.BlockSpec(memory_space=pl.ANY)],
                out_specs=pl.BlockSpec(memory_space=pltpu.VMEM),
                scratch_shapes=[
                    pltpu.VMEM((3 * rows, width), jnp.float32),
                    pltpu.VMEM((rows, width), jnp.bfloat16),
                    pltpu.VMEM((rows, width), jnp.bfloat16),
                    pltpu.SemaphoreType.DMA,
                    pltpu.SemaphoreType.DMA((CHUNKS,)),
                    pltpu.SemaphoreType.DMA((CHUNKS,)),
                    pltpu.SemaphoreType.DMA((CHUNKS,)),
                    pltpu.SemaphoreType.DMA((CHUNKS,)),
                ],
                compiler_params=pltpu.CompilerParams(
                    collective_id=value,
                    has_side_effects=True,
                    vmem_limit_bytes=32 * 1024 * 1024,
                ),
                cost_estimate=pl.CostEstimate(
                    flops=36 * rows * rows * width,
                    bytes_accessed=12 * rows * width,
                    transcendentals=0,
                ),
                name="mmd_mask_%d" % value,
            )(weights, features)

        return call

    return lax.switch(
        pick[0], [branch(value) for value in range(1, blocks - 1)], features, weights
    )


def tile_grad(own_rows, partner, weight, skip_diag):
    row_count, feat_width = own_rows.shape
    root_width = jnp.sqrt(jnp.float32(feat_width))
    scores = jnp.dot(own_rows, partner.T, precision=lax.Precision.HIGHEST) / root_width
    coefficient = weight * (6.0 / root_width) * (scores + 1.0) ** 2
    if skip_diag:
        coefficient = jnp.where(jnp.eye(row_count, dtype=bool), jnp.float32(0.0), coefficient)
    return jnp.dot(coefficient, partner, precision=lax.Precision.HIGHEST)


def permuted(values, axis, size, mask):
    def branch(value):
        pairs = [(at, at ^ value) for at in range(size)]
        return lambda values: lax.ppermute(values, axis, pairs)

    return lax.switch(mask, [branch(value) for value in range(size)], values)


def by_permutes(features, labels, rounds, across, down):
    blocks = across * down
    mask = jnp.bitwise_xor(jnp.bitwise_xor(rounds[0], rounds[1]), blocks - 1)
    own = lax.axis_index("gx") * down + lax.axis_index("gy")
    near = permuted(permuted(features, "gx", across, mask // down), "gy", down, mask % down)
    pairs = [(at, blocks - 1 - at) for at in range(blocks)]
    flip = lax.ppermute(features, ("gx", "gy"), pairs)
    all_rows = features.shape[0] * blocks
    real_rows = jnp.float32(features.shape[0]) * jnp.sum(labels).astype(jnp.float32)
    fake_rows = jnp.float32(all_rows) - real_rows
    loss_scale = float(all_rows) * float(all_rows) / 16.0

    def weight(other):
        return pair_weight(labels[own], labels[other], real_rows, fake_rows, loss_scale)

    return (
        tile_grad(features, features, weight(own), True)
        + tile_grad(features, near, weight(jnp.bitwise_xor(own, mask)), False)
        + tile_grad(features, flip, weight(blocks - 1 - own), False)
    )


def solution(mesh):
    across, down = mesh.shape["gx"], mesh.shape["gy"]
    blocks = across * down

    def on_device(features, labels, rounds):
        form = by_kernel if blocks <= KERNEL_DEVICES else by_permutes
        return form(features, labels, rounds, across, down)

    return jax.shard_map(
        on_device,
        mesh=mesh,
        in_specs=(P(("gx", "gy"), None), P(), P()),
        out_specs=P(("gx", "gy"), None),
        check_vma=False,
    )
```

```python
import functools

import jax
import jax.numpy as jnp
from jax import lax
from jax.experimental import pallas as pl
from jax.experimental.pallas import tpu as pltpu
from jax.sharding import PartitionSpec as P

MESH = pl.DeviceIdType.MESH
CHUNKS = 16
GROUPS = 4
STEP = 256
WINDOW = 6
DIRECT = 2
KERNEL_DEVICES = 64


def pair_weight(label_own, label_other, real_rows, fake_rows, loss_scale):
    both_real = loss_scale / (real_rows * (real_rows - 1.0))
    both_fake = loss_scale / (fake_rows * (fake_rows - 1.0))
    mixed = -loss_scale / (real_rows * fake_rows)
    same = label_own == label_other
    return jnp.where(same, jnp.where(label_own == 1, both_real, both_fake), mixed)


def flipped(index, mask):
    result = index
    bit = 1
    while bit <= mask:
        if mask & bit:
            result = result + bit * (1 - 2 * ((index // bit) % 2))
        bit *= 2
    return result


def split(values):
    high = values.astype(jnp.bfloat16)
    low = (values - high.astype(jnp.float32)).astype(jnp.bfloat16)
    return high, low


def dot_t(left, right):
    return lax.dot_general(
        left, right, (((1,), (1,)), ((), ())), preferred_element_type=jnp.float32
    )


def dot(left, right):
    return jnp.dot(left, right, preferred_element_type=jnp.float32)


def pick_kernel(across, down, rows, width, rounds_ref, labels_ref, pick_ref, weights_ref):
    blocks = across * down
    own = lax.axis_index("gx") * down + lax.axis_index("gy")
    mask = jnp.bitwise_xor(jnp.bitwise_xor(rounds_ref[0], rounds_ref[1]), blocks - 1)
    pick_ref[0] = mask - 1
    label_sum = lax.fori_loop(
        0, blocks, lambda at, total: total + labels_ref[at], jnp.int32(0)
    )
    all_rows = rows * blocks
    real_rows = (label_sum * rows).astype(jnp.float32)
    fake_rows = jnp.float32(all_rows) - real_rows
    loss_scale = float(all_rows) * float(all_rows) / 16.0
    label_own = labels_ref[own]
    others = (label_own, labels_ref[jnp.bitwise_xor(own, mask)], labels_ref[blocks - 1 - own])
    for at, label in enumerate(others):
        weight = pair_weight(label_own, label, real_rows, fake_rows, loss_scale)
        weights_ref[at] = weight * (6.0 / float(width) ** 0.5)


def exchange_kernel(
    mask, across, down, weights_ref, block_ref, grad_ref, held, own_high, own_low, part_high, part_low,
    load_sem, send_near, recv_near, send_far, recv_far,
):
    rows, width = block_ref.shape
    blocks = across * down
    crossing = 2 * mask >= blocks
    direct = 0 if crossing else DIRECT
    chunk = rows // CHUNKS
    group = rows // GROUPS
    per_group = CHUNKS // GROUPS
    own = lax.axis_index("gx") * down + lax.axis_index("gy")
    near = flipped(own, mask)
    far = flipped(own, (blocks - 1) ^ mask)
    flip = flipped(own, blocks - 1)
    peers = (near, far, flip) if direct else (near, far)

    def device(index):
        return (index // down, index % down)

    load = pltpu.make_async_copy(block_ref, held.at[pl.ds(0, rows)], load_sem)
    load.start()

    barrier = pltpu.get_barrier_semaphore()
    for peer in peers:
        pl.semaphore_signal(barrier, inc=1, device_id=device(peer), device_id_type=MESH)
    pl.semaphore_wait(barrier, len(peers))

    def to_near(at):
        return pltpu.make_async_remote_copy(
            src_ref=block_ref.at[pl.ds(at * chunk, chunk)],
            dst_ref=held.at[pl.ds(rows + at * chunk, chunk)],
            send_sem=send_near.at[at],
            recv_sem=recv_near.at[at],
            device_id=device(near),
            device_id_type=MESH,
        )

    def to_far(at):
        return pltpu.make_async_remote_copy(
            src_ref=held.at[pl.ds(rows + at * chunk, chunk)],
            dst_ref=held.at[pl.ds(2 * rows + at * chunk, chunk)],
            send_sem=send_far.at[at],
            recv_sem=recv_far.at[at],
            device_id=device(far),
            device_id_type=MESH,
        )

    def to_flip(at):
        return pltpu.make_async_remote_copy(
            src_ref=block_ref.at[pl.ds(at * chunk, chunk)],
            dst_ref=held.at[pl.ds(2 * rows + at * chunk, chunk)],
            send_sem=send_far.at[at],
            recv_sem=recv_far.at[at],
            device_id=device(flip),
            device_id_type=MESH,
        )

    def each(first, count, body):
        def step(at, carry):
            body(first + at)
            return carry

        lax.fori_loop(0, count, step, 0)

    for at in range(direct):
        to_flip(at).start()
    each(0, WINDOW, lambda at: to_near(at).start())

    load.wait()

    def prepare(at):
        here = pl.ds(at * group, group)
        high, low = split(held[here, :])
        own_high[here, :] = high
        own_low[here, :] = low
        grad_ref[here, :] = jnp.zeros((group, width), jnp.float32)

    each(0, GROUPS, prepare)

    def relay(at):
        to_near(at).wait_recv()

        @pl.when(at >= direct)
        def _():
            to_far(at).start()

        to_near(at).wait_send()

        @pl.when(at + WINDOW < CHUNKS)
        def _():
            to_near(at + WINDOW).start()

    def tile(at):
        if crossing:
            turn = at % 3
            which, place = 1 - turn + 3 * (turn // 2), at // 3
        else:
            last = at // (2 * GROUPS)
            which = (1 - last) * (1 - at % 2) + 2 * last
            place = (1 - last) * (at // 2) + last * (at - 2 * GROUPS)
        each(place * per_group, per_group * (which % 2), relay)
        each(
            place * per_group, per_group * (which // 2), lambda at: to_far(at).wait_recv()
        )
        high, low = split(held[pl.ds(which * rows + place * group, group), :])
        part_high[...] = high
        part_low[...] = low
        scores = (
            dot_t(own_high[...], high) + dot_t(own_high[...], low) + dot_t(own_low[...], high)
        ) * (1.0 / float(width) ** 0.5)
        raised = scores + 1.0
        coefficient = weights_ref[which] * (raised * raised)
        row = lax.broadcasted_iota(jnp.int32, (rows, group), 0)
        column = lax.broadcasted_iota(jnp.int32, (rows, group), 1) + (which * rows + place * group)
        coefficient = jnp.where(row == column, 0.0, coefficient)
        c_high, c_low = split(coefficient)

        def columns(at):
            here = pl.ds(pl.multiple_of(at * STEP, STEP), STEP)
            high, low = part_high[:, here], part_low[:, here]
            grad_ref[:, here] += dot(c_high, high) + dot(c_high, low) + dot(c_low, high)

        each(0, width // STEP, columns)

    each(0, 3 * GROUPS, tile)

    each(0, CHUNKS, lambda at: to_far(at).wait_send())


def by_kernel(features, labels, rounds, across, down):
    rows, width = features.shape
    blocks = across * down
    smem = pl.BlockSpec(memory_space=pltpu.SMEM)
    pick, weights = pl.pallas_call(
        functools.partial(pick_kernel, across, down, rows, width),
        out_shape=(
            jax.ShapeDtypeStruct((1,), jnp.int32),
            jax.ShapeDtypeStruct((3,), jnp.float32),
        ),
        in_specs=[smem, smem],
        out_specs=(smem, smem),
        compiler_params=pltpu.CompilerParams(vmem_limit_bytes=60 * 1024 * 1024),
        name="mmd_pick",
    )(rounds, labels)

    def branch(value):
        def call(features, weights):
            return pl.pallas_call(
                functools.partial(exchange_kernel, value, across, down),
                out_shape=jax.ShapeDtypeStruct((rows, width), jnp.float32),
                in_specs=[smem, pl.BlockSpec(memory_space=pl.ANY)],
                out_specs=pl.BlockSpec(memory_space=pltpu.VMEM),
                scratch_shapes=[
                    pltpu.VMEM((3 * rows, width), jnp.float32),
                    pltpu.VMEM((rows, width), jnp.bfloat16),
                    pltpu.VMEM((rows, width), jnp.bfloat16),
                    pltpu.VMEM((rows // GROUPS, width), jnp.bfloat16),
                    pltpu.VMEM((rows // GROUPS, width), jnp.bfloat16),
                    pltpu.SemaphoreType.DMA,
                    pltpu.SemaphoreType.DMA((CHUNKS,)),
                    pltpu.SemaphoreType.DMA((CHUNKS,)),
                    pltpu.SemaphoreType.DMA((CHUNKS,)),
                    pltpu.SemaphoreType.DMA((CHUNKS,)),
                ],
                compiler_params=pltpu.CompilerParams(
                    collective_id=value,
                    has_side_effects=True,
                    vmem_limit_bytes=32 * 1024 * 1024,
                ),
                cost_estimate=pl.CostEstimate(
                    flops=36 * rows * rows * width,
                    bytes_accessed=12 * rows * width,
                    transcendentals=0,
                ),
                name="mmd_mask_%d" % value,
            )(weights, features)

        return call

    return lax.switch(
        pick[0], [branch(value) for value in range(1, blocks - 1)], features, weights
    )


def tile_grad(own_rows, partner, weight, skip_diag):
    row_count, feat_width = own_rows.shape
    root_width = jnp.sqrt(jnp.float32(feat_width))
    scores = jnp.dot(own_rows, partner.T, precision=lax.Precision.HIGHEST) / root_width
    coefficient = weight * (6.0 / root_width) * (scores + 1.0) ** 2
    if skip_diag:
        coefficient = jnp.where(jnp.eye(row_count, dtype=bool), jnp.float32(0.0), coefficient)
    return jnp.dot(coefficient, partner, precision=lax.Precision.HIGHEST)


def permuted(values, axis, size, mask):
    def branch(value):
        pairs = [(at, at ^ value) for at in range(size)]
        return lambda values: lax.ppermute(values, axis, pairs)

    return lax.switch(mask, [branch(value) for value in range(size)], values)


def by_permutes(features, labels, rounds, across, down):
    blocks = across * down
    mask = jnp.bitwise_xor(jnp.bitwise_xor(rounds[0], rounds[1]), blocks - 1)
    own = lax.axis_index("gx") * down + lax.axis_index("gy")
    near = permuted(permuted(features, "gx", across, mask // down), "gy", down, mask % down)
    pairs = [(at, blocks - 1 - at) for at in range(blocks)]
    flip = lax.ppermute(features, ("gx", "gy"), pairs)
    all_rows = features.shape[0] * blocks
    real_rows = jnp.float32(features.shape[0]) * jnp.sum(labels).astype(jnp.float32)
    fake_rows = jnp.float32(all_rows) - real_rows
    loss_scale = float(all_rows) * float(all_rows) / 16.0

    def weight(other):
        return pair_weight(labels[own], labels[other], real_rows, fake_rows, loss_scale)

    return (
        tile_grad(features, features, weight(own), True)
        + tile_grad(features, near, weight(jnp.bitwise_xor(own, mask)), False)
        + tile_grad(features, flip, weight(blocks - 1 - own), False)
    )


def solution(mesh):
    across, down = mesh.shape["gx"], mesh.shape["gy"]
    blocks = across * down

    def on_device(features, labels, rounds):
        form = by_kernel if blocks <= KERNEL_DEVICES else by_permutes
        return form(features, labels, rounds, across, down)

    return jax.shard_map(
        on_device,
        mesh=mesh,
        in_specs=(P(("gx", "gy"), None), P(), P()),
        out_specs=P(("gx", "gy"), None),
        check_vma=False,
    )
```

```python
import functools

import jax
import jax.numpy as jnp
from jax import lax
from jax.experimental import pallas as pl
from jax.experimental.pallas import tpu as pltpu
from jax.sharding import PartitionSpec as P

MESH = pl.DeviceIdType.MESH
CHUNKS = 8
GROUPS = 4
STEP = 256
KERNEL_DEVICES = 64


def pair_weight(label_own, label_other, real_rows, fake_rows, loss_scale):
    both_real = loss_scale / (real_rows * (real_rows - 1.0))
    both_fake = loss_scale / (fake_rows * (fake_rows - 1.0))
    mixed = -loss_scale / (real_rows * fake_rows)
    same = label_own == label_other
    return jnp.where(same, jnp.where(label_own == 1, both_real, both_fake), mixed)


def flipped(index, mask):
    result = index
    bit = 1
    while bit <= mask:
        if mask & bit:
            result = result + bit * (1 - 2 * ((index // bit) % 2))
        bit *= 2
    return result


def split(values):
    high = values.astype(jnp.bfloat16)
    low = (values - high.astype(jnp.float32)).astype(jnp.bfloat16)
    return high, low


def dot_t(left, right):
    return lax.dot_general(
        left, right, (((1,), (1,)), ((), ())), preferred_element_type=jnp.float32
    )


def dot(left, right):
    return jnp.dot(left, right, preferred_element_type=jnp.float32)


def pick_kernel(across, down, rows, width, rounds_ref, labels_ref, pick_ref, weights_ref):
    blocks = across * down
    own = lax.axis_index("gx") * down + lax.axis_index("gy")
    mask = jnp.bitwise_xor(jnp.bitwise_xor(rounds_ref[0], rounds_ref[1]), blocks - 1)
    pick_ref[0] = mask - 1
    label_sum = lax.fori_loop(
        0, blocks, lambda at, total: total + labels_ref[at], jnp.int32(0)
    )
    all_rows = rows * blocks
    real_rows = (label_sum * rows).astype(jnp.float32)
    fake_rows = jnp.float32(all_rows) - real_rows
    loss_scale = float(all_rows) * float(all_rows) / 16.0
    label_own = labels_ref[own]
    others = (label_own, labels_ref[jnp.bitwise_xor(own, mask)], labels_ref[blocks - 1 - own])
    for at, label in enumerate(others):
        weight = pair_weight(label_own, label, real_rows, fake_rows, loss_scale)
        weights_ref[at] = weight * (6.0 / float(width) ** 0.5)


def exchange_kernel(
    mask, across, down, weights_ref, block_ref, grad_ref, held, own_high, own_low, part_high, part_low,
    load_sem, send_near, recv_near, send_far, recv_far,
):
    rows, width = block_ref.shape
    blocks = across * down
    crossing = 2 * mask >= blocks
    chunk = rows // CHUNKS
    group = rows // GROUPS
    per_group = CHUNKS // GROUPS
    own = lax.axis_index("gx") * down + lax.axis_index("gy")
    near = flipped(own, mask)
    far = flipped(own, (blocks - 1) ^ mask if crossing else blocks - 1)
    peers = (near, far)

    def device(index):
        return (index // down, index % down)

    load = pltpu.make_async_copy(block_ref, held.at[pl.ds(0, rows)], load_sem)
    load.start()

    barrier = pltpu.get_barrier_semaphore()
    for peer in peers:
        pl.semaphore_signal(barrier, inc=1, device_id=device(peer), device_id_type=MESH)
    pl.semaphore_wait(barrier, len(peers))

    def to_near(at):
        return pltpu.make_async_remote_copy(
            src_ref=block_ref.at[pl.ds(at * chunk, chunk)],
            dst_ref=held.at[pl.ds(rows + at * chunk, chunk)],
            send_sem=send_near.at[at],
            recv_sem=recv_near.at[at],
            device_id=device(near),
            device_id_type=MESH,
        )

    def to_far(at):
        source = held.at[pl.ds(rows + at * chunk, chunk)] if crossing else (
            block_ref.at[pl.ds(at * chunk, chunk)]
        )
        return pltpu.make_async_remote_copy(
            src_ref=source,
            dst_ref=held.at[pl.ds(2 * rows + at * chunk, chunk)],
            send_sem=send_far.at[at],
            recv_sem=recv_far.at[at],
            device_id=device(far),
            device_id_type=MESH,
        )

    def each(first, count, body):
        def step(at, carry):
            body(first + at)
            return carry

        lax.fori_loop(0, count, step, 0)

    if not crossing:
        each(0, CHUNKS, lambda at: to_far(at).start())
    each(0, CHUNKS, lambda at: to_near(at).start())

    load.wait()

    def prepare(at):
        here = pl.ds(at * group, group)
        high, low = split(held[here, :])
        own_high[here, :] = high
        own_low[here, :] = low
        grad_ref[here, :] = jnp.zeros((group, width), jnp.float32)

    each(0, GROUPS, prepare)

    def relay(at):
        to_near(at).wait_recv()
        if crossing:
            to_far(at).start()

    def tile(at):
        which, place = at // GROUPS, at % GROUPS
        each(place * per_group, per_group * (which % 2), relay)
        each(
            place * per_group, per_group * (which // 2), lambda at: to_far(at).wait_recv()
        )
        high, low = split(held[pl.ds(which * rows + place * group, group), :])
        part_high[...] = high
        part_low[...] = low
        scores = (
            dot_t(own_high[...], high) + dot_t(own_high[...], low) + dot_t(own_low[...], high)
        ) * (1.0 / float(width) ** 0.5)
        raised = scores + 1.0
        coefficient = weights_ref[which] * (raised * raised)
        row = lax.broadcasted_iota(jnp.int32, (rows, group), 0)
        column = lax.broadcasted_iota(jnp.int32, (rows, group), 1) + (which * rows + place * group)
        coefficient = jnp.where(row == column, 0.0, coefficient)
        c_high, c_low = split(coefficient)

        def columns(at):
            here = pl.ds(pl.multiple_of(at * STEP, STEP), STEP)
            high, low = part_high[:, here], part_low[:, here]
            grad_ref[:, here] += dot(c_high, high) + dot(c_high, low) + dot(c_low, high)

        each(0, width // STEP, columns)

    each(0, 3 * GROUPS, tile)

    def finish(at):
        to_near(at).wait_send()
        to_far(at).wait_send()

    each(0, CHUNKS, finish)


def by_kernel(features, labels, rounds, across, down):
    rows, width = features.shape
    blocks = across * down
    smem = pl.BlockSpec(memory_space=pltpu.SMEM)
    pick, weights = pl.pallas_call(
        functools.partial(pick_kernel, across, down, rows, width),
        out_shape=(
            jax.ShapeDtypeStruct((1,), jnp.int32),
            jax.ShapeDtypeStruct((3,), jnp.float32),
        ),
        in_specs=[smem, smem],
        out_specs=(smem, smem),
        compiler_params=pltpu.CompilerParams(vmem_limit_bytes=60 * 1024 * 1024),
        name="mmd_pick",
    )(rounds, labels)

    def branch(value):
        def call(features, weights):
            return pl.pallas_call(
                functools.partial(exchange_kernel, value, across, down),
                out_shape=jax.ShapeDtypeStruct((rows, width), jnp.float32),
                in_specs=[smem, pl.BlockSpec(memory_space=pl.ANY)],
                out_specs=pl.BlockSpec(memory_space=pltpu.VMEM),
                scratch_shapes=[
                    pltpu.VMEM((3 * rows, width), jnp.float32),
                    pltpu.VMEM((rows, width), jnp.bfloat16),
                    pltpu.VMEM((rows, width), jnp.bfloat16),
                    pltpu.VMEM((rows // GROUPS, width), jnp.bfloat16),
                    pltpu.VMEM((rows // GROUPS, width), jnp.bfloat16),
                    pltpu.SemaphoreType.DMA,
                    pltpu.SemaphoreType.DMA((CHUNKS,)),
                    pltpu.SemaphoreType.DMA((CHUNKS,)),
                    pltpu.SemaphoreType.DMA((CHUNKS,)),
                    pltpu.SemaphoreType.DMA((CHUNKS,)),
                ],
                compiler_params=pltpu.CompilerParams(
                    collective_id=value,
                    has_side_effects=True,
                    vmem_limit_bytes=32 * 1024 * 1024,
                ),
                cost_estimate=pl.CostEstimate(
                    flops=36 * rows * rows * width,
                    bytes_accessed=12 * rows * width,
                    transcendentals=0,
                ),
                name="mmd_mask_%d" % value,
            )(weights, features)

        return call

    return lax.switch(
        pick[0], [branch(value) for value in range(1, blocks - 1)], features, weights
    )


def tile_grad(own_rows, partner, weight, skip_diag):
    row_count, feat_width = own_rows.shape
    root_width = jnp.sqrt(jnp.float32(feat_width))
    scores = jnp.dot(own_rows, partner.T, precision=lax.Precision.HIGHEST) / root_width
    coefficient = weight * (6.0 / root_width) * (scores + 1.0) ** 2
    if skip_diag:
        coefficient = jnp.where(jnp.eye(row_count, dtype=bool), jnp.float32(0.0), coefficient)
    return jnp.dot(coefficient, partner, precision=lax.Precision.HIGHEST)


def permuted(values, axis, size, mask):
    def branch(value):
        pairs = [(at, at ^ value) for at in range(size)]
        return lambda values: lax.ppermute(values, axis, pairs)

    return lax.switch(mask, [branch(value) for value in range(size)], values)


def by_permutes(features, labels, rounds, across, down):
    blocks = across * down
    mask = jnp.bitwise_xor(jnp.bitwise_xor(rounds[0], rounds[1]), blocks - 1)
    own = lax.axis_index("gx") * down + lax.axis_index("gy")
    near = permuted(permuted(features, "gx", across, mask // down), "gy", down, mask % down)
    pairs = [(at, blocks - 1 - at) for at in range(blocks)]
    flip = lax.ppermute(features, ("gx", "gy"), pairs)
    all_rows = features.shape[0] * blocks
    real_rows = jnp.float32(features.shape[0]) * jnp.sum(labels).astype(jnp.float32)
    fake_rows = jnp.float32(all_rows) - real_rows
    loss_scale = float(all_rows) * float(all_rows) / 16.0

    def weight(other):
        return pair_weight(labels[own], labels[other], real_rows, fake_rows, loss_scale)

    return (
        tile_grad(features, features, weight(own), True)
        + tile_grad(features, near, weight(jnp.bitwise_xor(own, mask)), False)
        + tile_grad(features, flip, weight(blocks - 1 - own), False)
    )


def solution(mesh):
    across, down = mesh.shape["gx"], mesh.shape["gy"]
    blocks = across * down

    def on_device(features, labels, rounds):
        form = by_kernel if blocks <= KERNEL_DEVICES else by_permutes
        return form(features, labels, rounds, across, down)

    return jax.shard_map(
        on_device,
        mesh=mesh,
        in_specs=(P(("gx", "gy"), None), P(), P()),
        out_specs=P(("gx", "gy"), None),
        check_vma=False,
    )
```

```python
import functools

import jax
import jax.numpy as jnp
from jax import lax
from jax.experimental import pallas as pl
from jax.experimental.pallas import tpu as pltpu
from jax.sharding import PartitionSpec as P

MESH = pl.DeviceIdType.MESH
CHUNKS = 8
GROUPS = 2
STEP = 256
SLAB = 32
DIRECT = 1
KERNEL_DEVICES = 64


def pair_weight(label_own, label_other, real_rows, fake_rows, loss_scale):
    both_real = loss_scale / (real_rows * (real_rows - 1.0))
    both_fake = loss_scale / (fake_rows * (fake_rows - 1.0))
    mixed = -loss_scale / (real_rows * fake_rows)
    same = label_own == label_other
    return jnp.where(same, jnp.where(label_own == 1, both_real, both_fake), mixed)


def flipped(index, mask):
    result = index
    bit = 1
    while bit <= mask:
        if mask & bit:
            result = result + bit * (1 - 2 * ((index // bit) % 2))
        bit *= 2
    return result


def split(values):
    high = values.astype(jnp.bfloat16)
    low = (values - high.astype(jnp.float32)).astype(jnp.bfloat16)
    return high, low


def dot_t(left, right):
    return lax.dot_general(
        left, right, (((1,), (1,)), ((), ())), preferred_element_type=jnp.float32
    )


def dot(left, right):
    return jnp.dot(left, right, preferred_element_type=jnp.float32)


def pick_kernel(across, down, rows, width, rounds_ref, labels_ref, pick_ref, weights_ref):
    blocks = across * down
    own = lax.axis_index("gx") * down + lax.axis_index("gy")
    mask = jnp.bitwise_xor(jnp.bitwise_xor(rounds_ref[0], rounds_ref[1]), blocks - 1)
    pick_ref[0] = mask - 1
    label_sum = lax.fori_loop(
        0, blocks, lambda at, total: total + labels_ref[at], jnp.int32(0)
    )
    all_rows = rows * blocks
    real_rows = (label_sum * rows).astype(jnp.float32)
    fake_rows = jnp.float32(all_rows) - real_rows
    loss_scale = float(all_rows) * float(all_rows) / 16.0
    label_own = labels_ref[own]
    others = (label_own, labels_ref[jnp.bitwise_xor(own, mask)], labels_ref[blocks - 1 - own])
    for at, label in enumerate(others):
        weight = pair_weight(label_own, label, real_rows, fake_rows, loss_scale)
        weights_ref[at] = weight * (6.0 / float(width) ** 0.5)


def exchange_kernel(
    mask, across, down, weights_ref, block_ref, grad_ref, held, own_high, own_low, part, both,
    load_sem, send_near, recv_near, send_far, recv_far,
):
    rows, width = block_ref.shape
    blocks = across * down
    crossing = 2 * mask >= blocks
    chunk = rows // CHUNKS
    group = rows // GROUPS
    per_group = CHUNKS // GROUPS
    own = lax.axis_index("gx") * down + lax.axis_index("gy")
    near = flipped(own, mask)
    far = flipped(own, (blocks - 1) ^ mask)
    flip = flipped(own, blocks - 1)
    direct = 0 if crossing else DIRECT
    peers = (near, far, flip) if direct else (near, far)

    def device(index):
        return (index // down, index % down)

    load = pltpu.make_async_copy(block_ref, held.at[pl.ds(0, rows)], load_sem)
    load.start()

    barrier = pltpu.get_barrier_semaphore()
    for peer in peers:
        pl.semaphore_signal(barrier, inc=1, device_id=device(peer), device_id_type=MESH)
    pl.semaphore_wait(barrier, len(peers))

    def to_near(at):
        return pltpu.make_async_remote_copy(
            src_ref=block_ref.at[pl.ds(at * chunk, chunk)],
            dst_ref=held.at[pl.ds(rows + at * chunk, chunk)],
            send_sem=send_near.at[at],
            recv_sem=recv_near.at[at],
            device_id=device(near),
            device_id_type=MESH,
        )

    def to_far(at):
        return pltpu.make_async_remote_copy(
            src_ref=held.at[pl.ds(rows + at * chunk, chunk)],
            dst_ref=held.at[pl.ds(2 * rows + at * chunk, chunk)],
            send_sem=send_far.at[at],
            recv_sem=recv_far.at[at],
            device_id=device(far),
            device_id_type=MESH,
        )

    def to_flip(at):
        return pltpu.make_async_remote_copy(
            src_ref=block_ref.at[pl.ds(at * chunk, chunk)],
            dst_ref=held.at[pl.ds(2 * rows + at * chunk, chunk)],
            send_sem=send_far.at[at],
            recv_sem=recv_far.at[at],
            device_id=device(flip),
            device_id_type=MESH,
        )

    def each(first, count, body):
        def step(at, carry):
            body(first + at)
            return carry

        lax.fori_loop(0, count, step, 0)

    each(0, CHUNKS, lambda at: to_near(at).start())
    for at in range(direct):
        to_flip(at).start()

    load.wait()

    def prepare(at):
        here = pl.ds(at * SLAB, SLAB)
        high, low = split(held[here, :])
        own_high[here, :] = high
        own_low[here, :] = low
        grad_ref[here, :] = jnp.zeros((SLAB, width), jnp.float32)

    each(0, rows // SLAB, prepare)

    def relay(at):
        to_near(at).wait_recv()

        @pl.when(at >= direct)
        def _():
            to_far(at).start()

    def tile(at):
        past = (at // GROUPS + 1) // 2
        later = at - GROUPS
        if crossing:
            which, place = past * (1 + later % 2), past * (later // 2)
        else:
            which, place = past * (1 + later // GROUPS), past * (later % GROUPS)
        place = place + (1 - past) * at
        each(place * per_group, per_group * (which % 2), relay)
        each(
            place * per_group, per_group * (which // 2), lambda at: to_far(at).wait_recv()
        )

        def split_part(at):
            high, low = split(held[pl.ds(which * rows + place * group + at * SLAB, SLAB), :])
            part[pl.ds(at * SLAB, SLAB), :] = high
            part[pl.ds(group + at * SLAB, SLAB), :] = low

        each(0, group // SLAB, split_part)
        both[...] = jnp.zeros((rows, 2 * group), jnp.float32)

        def depth(at):
            here = pl.ds(pl.multiple_of(at * STEP, STEP), STEP)
            both[...] += dot_t(own_high[:, here], part[:, here])
            both[:, 0:group] += dot_t(own_low[:, here], part[0:group, here])

        each(0, width // STEP, depth)
        scores = both[:, 0:group] + both[:, group:]
        raised = scores * (1.0 / float(width) ** 0.5) + 1.0
        coefficient = weights_ref[which] * (raised * raised)
        row = lax.broadcasted_iota(jnp.int32, (rows, group), 0)
        column = lax.broadcasted_iota(jnp.int32, (rows, group), 1) + (which * rows + place * group)
        coefficient = jnp.where(row == column, 0.0, coefficient)
        c_high, c_low = split(coefficient)
        c_twice = jnp.concatenate([c_high, c_high], axis=1)

        def columns(at):
            here = pl.ds(pl.multiple_of(at * STEP, STEP), STEP)
            grad_ref[:, here] += dot(c_twice, part[:, here]) + dot(c_low, part[0:group, here])

        each(0, width // STEP, columns)

    each(0, 3 * GROUPS, tile)

    def finish(at):
        to_near(at).wait_send()
        to_far(at).wait_send()

    each(0, CHUNKS, finish)


def by_kernel(features, labels, rounds, across, down):
    rows, width = features.shape
    blocks = across * down
    smem = pl.BlockSpec(memory_space=pltpu.SMEM)
    pick, weights = pl.pallas_call(
        functools.partial(pick_kernel, across, down, rows, width),
        out_shape=(
            jax.ShapeDtypeStruct((1,), jnp.int32),
            jax.ShapeDtypeStruct((3,), jnp.float32),
        ),
        in_specs=[smem, smem],
        out_specs=(smem, smem),
        compiler_params=pltpu.CompilerParams(vmem_limit_bytes=60 * 1024 * 1024),
        name="mmd_pick",
    )(rounds, labels)

    def branch(value):
        def call(features, weights):
            return pl.pallas_call(
                functools.partial(exchange_kernel, value, across, down),
                out_shape=jax.ShapeDtypeStruct((rows, width), jnp.float32),
                in_specs=[smem, pl.BlockSpec(memory_space=pl.ANY)],
                out_specs=pl.BlockSpec(memory_space=pltpu.VMEM),
                scratch_shapes=[
                    pltpu.VMEM((3 * rows, width), jnp.float32),
                    pltpu.VMEM((rows, width), jnp.bfloat16),
                    pltpu.VMEM((rows, width), jnp.bfloat16),
                    pltpu.VMEM((2 * rows // GROUPS, width), jnp.bfloat16),
                    pltpu.VMEM((rows, 2 * rows // GROUPS), jnp.float32),
                    pltpu.SemaphoreType.DMA,
                    pltpu.SemaphoreType.DMA((CHUNKS,)),
                    pltpu.SemaphoreType.DMA((CHUNKS,)),
                    pltpu.SemaphoreType.DMA((CHUNKS,)),
                    pltpu.SemaphoreType.DMA((CHUNKS,)),
                ],
                compiler_params=pltpu.CompilerParams(
                    collective_id=value,
                    has_side_effects=True,
                    vmem_limit_bytes=32 * 1024 * 1024,
                ),
                cost_estimate=pl.CostEstimate(
                    flops=36 * rows * rows * width,
                    bytes_accessed=12 * rows * width,
                    transcendentals=0,
                ),
                name="mmd_mask_%d" % value,
            )(weights, features)

        return call

    return lax.switch(
        pick[0], [branch(value) for value in range(1, blocks - 1)], features, weights
    )


def tile_grad(own_rows, partner, weight, skip_diag):
    row_count, feat_width = own_rows.shape
    root_width = jnp.sqrt(jnp.float32(feat_width))
    scores = jnp.dot(own_rows, partner.T, precision=lax.Precision.HIGHEST) / root_width
    coefficient = weight * (6.0 / root_width) * (scores + 1.0) ** 2
    if skip_diag:
        coefficient = jnp.where(jnp.eye(row_count, dtype=bool), jnp.float32(0.0), coefficient)
    return jnp.dot(coefficient, partner, precision=lax.Precision.HIGHEST)


def permuted(values, axis, size, mask):
    def branch(value):
        pairs = [(at, at ^ value) for at in range(size)]
        return lambda values: lax.ppermute(values, axis, pairs)

    return lax.switch(mask, [branch(value) for value in range(size)], values)


def by_permutes(features, labels, rounds, across, down):
    blocks = across * down
    mask = jnp.bitwise_xor(jnp.bitwise_xor(rounds[0], rounds[1]), blocks - 1)
    own = lax.axis_index("gx") * down + lax.axis_index("gy")
    near = permuted(permuted(features, "gx", across, mask // down), "gy", down, mask % down)
    pairs = [(at, blocks - 1 - at) for at in range(blocks)]
    flip = lax.ppermute(features, ("gx", "gy"), pairs)
    all_rows = features.shape[0] * blocks
    real_rows = jnp.float32(features.shape[0]) * jnp.sum(labels).astype(jnp.float32)
    fake_rows = jnp.float32(all_rows) - real_rows
    loss_scale = float(all_rows) * float(all_rows) / 16.0

    def weight(other):
        return pair_weight(labels[own], labels[other], real_rows, fake_rows, loss_scale)

    return (
        tile_grad(features, features, weight(own), True)
        + tile_grad(features, near, weight(jnp.bitwise_xor(own, mask)), False)
        + tile_grad(features, flip, weight(blocks - 1 - own), False)
    )


def solution(mesh):
    across, down = mesh.shape["gx"], mesh.shape["gy"]
    blocks = across * down

    def on_device(features, labels, rounds):
        form = by_kernel if blocks <= KERNEL_DEVICES else by_permutes
        return form(features, labels, rounds, across, down)

    return jax.shard_map(
        on_device,
        mesh=mesh,
        in_specs=(P(("gx", "gy"), None), P(), P()),
        out_specs=P(("gx", "gy"), None),
        check_vma=False,
    )
```

```python
import functools

import jax
import jax.numpy as jnp
from jax import lax
from jax.experimental import pallas as pl
from jax.experimental.pallas import tpu as pltpu
from jax.sharding import PartitionSpec as P

MESH = pl.DeviceIdType.MESH
CHUNKS = 8
GROUPS = 2
STEP = 256
SLAB = 32
DIRECT = 1
KERNEL_DEVICES = 64


def pair_weight(label_own, label_other, real_rows, fake_rows, loss_scale):
    both_real = loss_scale / (real_rows * (real_rows - 1.0))
    both_fake = loss_scale / (fake_rows * (fake_rows - 1.0))
    mixed = -loss_scale / (real_rows * fake_rows)
    same = label_own == label_other
    return jnp.where(same, jnp.where(label_own == 1, both_real, both_fake), mixed)


def flipped(index, mask):
    result = index
    bit = 1
    while bit <= mask:
        if mask & bit:
            result = result + bit * (1 - 2 * ((index // bit) % 2))
        bit *= 2
    return result


def split(values):
    high = values.astype(jnp.bfloat16)
    low = (values - high.astype(jnp.float32)).astype(jnp.bfloat16)
    return high, low


def dot_t(left, right):
    return lax.dot_general(
        left, right, (((1,), (1,)), ((), ())), preferred_element_type=jnp.float32
    )


def dot(left, right):
    return jnp.dot(left, right, preferred_element_type=jnp.float32)


def pick_kernel(across, down, rows, width, rounds_ref, labels_ref, pick_ref, weights_ref):
    blocks = across * down
    own = lax.axis_index("gx") * down + lax.axis_index("gy")
    mask = jnp.bitwise_xor(jnp.bitwise_xor(rounds_ref[0], rounds_ref[1]), blocks - 1)
    pick_ref[0] = mask - 1
    label_sum = lax.fori_loop(
        0, blocks, lambda at, total: total + labels_ref[at], jnp.int32(0)
    )
    all_rows = rows * blocks
    real_rows = (label_sum * rows).astype(jnp.float32)
    fake_rows = jnp.float32(all_rows) - real_rows
    loss_scale = float(all_rows) * float(all_rows) / 16.0
    label_own = labels_ref[own]
    others = (label_own, labels_ref[jnp.bitwise_xor(own, mask)], labels_ref[blocks - 1 - own])
    for at, label in enumerate(others):
        weight = pair_weight(label_own, label, real_rows, fake_rows, loss_scale)
        weights_ref[at] = weight * (6.0 / float(width) ** 0.5)


def exchange_kernel(
    mask, across, down, weights_ref, block_ref, grad_ref, held, own_high, own_low, part, both, factor,
    load_sem, send_near, recv_near, send_far, recv_far, send_flip,
):
    rows, width = block_ref.shape
    blocks = across * down
    crossing = 2 * mask >= blocks
    chunk = rows // CHUNKS
    group = rows // GROUPS
    per_group = CHUNKS // GROUPS
    own = lax.axis_index("gx") * down + lax.axis_index("gy")
    near = flipped(own, mask)
    far = flipped(own, (blocks - 1) ^ mask)
    flip = flipped(own, blocks - 1)
    middle = not crossing and 4 * mask >= blocks
    in_middle = (own // (blocks // 2) + own // (blocks // 4)) % 2 == 1
    direct = 0 if crossing or middle else DIRECT
    peers = (near, far) if crossing else (near, far, flip)

    def device(index):
        return (index // down, index % down)

    load = pltpu.make_async_copy(block_ref, held.at[pl.ds(0, rows)], load_sem)
    load.start()

    barrier = pltpu.get_barrier_semaphore()
    for peer in peers:
        pl.semaphore_signal(barrier, inc=1, device_id=device(peer), device_id_type=MESH)
    pl.semaphore_wait(barrier, len(peers))

    def to_near(at):
        return pltpu.make_async_remote_copy(
            src_ref=block_ref.at[pl.ds(at * chunk, chunk)],
            dst_ref=held.at[pl.ds(rows + at * chunk, chunk)],
            send_sem=send_near.at[at],
            recv_sem=recv_near.at[at],
            device_id=device(near),
            device_id_type=MESH,
        )

    def to_far(at):
        return pltpu.make_async_remote_copy(
            src_ref=held.at[pl.ds(rows + at * chunk, chunk)],
            dst_ref=held.at[pl.ds(2 * rows + at * chunk, chunk)],
            send_sem=send_far.at[at],
            recv_sem=recv_far.at[at],
            device_id=device(far),
            device_id_type=MESH,
        )

    def to_flip(at):
        return pltpu.make_async_remote_copy(
            src_ref=block_ref.at[pl.ds(at * chunk, chunk)],
            dst_ref=held.at[pl.ds(2 * rows + at * chunk, chunk)],
            send_sem=send_flip.at[at] if middle else send_far.at[at],
            recv_sem=recv_far.at[at],
            device_id=device(flip),
            device_id_type=MESH,
        )

    def each(first, count, body):
        def step(at, carry):
            body(first + at)
            return carry

        lax.fori_loop(0, count, step, 0)

    each(0, CHUNKS, lambda at: to_near(at).start())
    for at in range(direct):
        to_flip(at).start()
    if middle:

        @pl.when(in_middle)
        def _():
            each(0, CHUNKS, lambda at: to_flip(at).start())

    load.wait()

    def prepare(at):
        here = pl.ds(at * SLAB, SLAB)
        high, low = split(held[here, :])
        own_high[here, :] = high
        own_low[here, :] = low
        grad_ref[here, :] = jnp.zeros((SLAB, width), jnp.float32)

    each(0, rows // SLAB, prepare)

    def relay(at):
        to_near(at).wait_recv()

        @pl.when(in_middle if middle else at >= direct)
        def _():
            to_far(at).start()

    def tile(at):
        past = (at // GROUPS + 1) // 2
        later = at - GROUPS
        if crossing:
            which, place = past * (1 + later % 2), past * (later // 2)
        else:
            which, place = past * (1 + later // GROUPS), past * (later % GROUPS)
        place = place + (1 - past) * at
        each(place * per_group, per_group * (which % 2), relay)
        each(
            place * per_group, per_group * (which // 2), lambda at: to_far(at).wait_recv()
        )

        def split_part(at):
            high, low = split(held[pl.ds(which * rows + place * group + at * SLAB, SLAB), :])
            part[pl.ds(at * SLAB, SLAB), :] = high
            part[pl.ds(group + at * SLAB, SLAB), :] = low

        each(0, group // SLAB, split_part)
        both[...] = jnp.zeros((rows, 2 * group), jnp.float32)

        def depth(at):
            here = pl.ds(pl.multiple_of(at * STEP, STEP), STEP)
            both[...] += dot_t(own_high[:, here], part[:, here])
            both[:, 0:group] += dot_t(own_low[:, here], part[0:group, here])

        each(0, width // STEP, depth)

        def coefficients(at):
            here = pl.ds(at * SLAB, SLAB)
            scores = both[here, 0:group] + both[here, group:]
            raised = scores * (1.0 / float(width) ** 0.5) + 1.0
            coefficient = weights_ref[which] * (raised * raised)
            row = lax.broadcasted_iota(jnp.int32, (SLAB, group), 0) + at * SLAB
            column = lax.broadcasted_iota(jnp.int32, (SLAB, group), 1)
            column = column + (which * rows + place * group)
            coefficient = jnp.where(row == column, 0.0, coefficient)
            high, low = split(coefficient)
            factor[here, 0:group] = high
            factor[here, group : 2 * group] = high
            factor[here, 2 * group :] = low

        each(0, rows // SLAB, coefficients)

        def columns(at):
            here = pl.ds(pl.multiple_of(at * STEP, STEP), STEP)
            grad_ref[:, here] += dot(factor[:, 0 : 2 * group], part[:, here]) + dot(
                factor[:, 2 * group :], part[0:group, here]
            )

        each(0, width // STEP, columns)

    each(0, 3 * GROUPS, tile)

    def finish(at):
        to_near(at).wait_send()
        if middle:

            @pl.when(in_middle)
            def _():
                to_far(at).wait_send()
                to_flip(at).wait_send()
        else:
            to_far(at).wait_send()

    each(0, CHUNKS, finish)


def by_kernel(features, labels, rounds, across, down):
    rows, width = features.shape
    blocks = across * down
    smem = pl.BlockSpec(memory_space=pltpu.SMEM)
    pick, weights = pl.pallas_call(
        functools.partial(pick_kernel, across, down, rows, width),
        out_shape=(
            jax.ShapeDtypeStruct((1,), jnp.int32),
            jax.ShapeDtypeStruct((3,), jnp.float32),
        ),
        in_specs=[smem, smem],
        out_specs=(smem, smem),
        compiler_params=pltpu.CompilerParams(vmem_limit_bytes=60 * 1024 * 1024),
        name="mmd_pick",
    )(rounds, labels)

    def branch(value):
        def call(features, weights):
            return pl.pallas_call(
                functools.partial(exchange_kernel, value, across, down),
                out_shape=jax.ShapeDtypeStruct((rows, width), jnp.float32),
                in_specs=[smem, pl.BlockSpec(memory_space=pl.ANY)],
                out_specs=pl.BlockSpec(memory_space=pltpu.VMEM),
                scratch_shapes=[
                    pltpu.VMEM((3 * rows, width), jnp.float32),
                    pltpu.VMEM((rows, width), jnp.bfloat16),
                    pltpu.VMEM((rows, width), jnp.bfloat16),
                    pltpu.VMEM((2 * rows // GROUPS, width), jnp.bfloat16),
                    pltpu.VMEM((rows, 2 * rows // GROUPS), jnp.float32),
                    pltpu.VMEM((rows, 3 * rows // GROUPS), jnp.bfloat16),
                    pltpu.SemaphoreType.DMA,
                    pltpu.SemaphoreType.DMA((CHUNKS,)),
                    pltpu.SemaphoreType.DMA((CHUNKS,)),
                    pltpu.SemaphoreType.DMA((CHUNKS,)),
                    pltpu.SemaphoreType.DMA((CHUNKS,)),
                    pltpu.SemaphoreType.DMA((CHUNKS,)),
                ],
                compiler_params=pltpu.CompilerParams(
                    collective_id=value,
                    has_side_effects=True,
                    vmem_limit_bytes=32 * 1024 * 1024,
                ),
                cost_estimate=pl.CostEstimate(
                    flops=36 * rows * rows * width,
                    bytes_accessed=12 * rows * width,
                    transcendentals=0,
                ),
                name="mmd_mask_%d" % value,
            )(weights, features)

        return call

    return lax.switch(
        pick[0], [branch(value) for value in range(1, blocks - 1)], features, weights
    )


def tile_grad(own_rows, partner, weight, skip_diag):
    row_count, feat_width = own_rows.shape
    root_width = jnp.sqrt(jnp.float32(feat_width))
    scores = jnp.dot(own_rows, partner.T, precision=lax.Precision.HIGHEST) / root_width
    coefficient = weight * (6.0 / root_width) * (scores + 1.0) ** 2
    if skip_diag:
        coefficient = jnp.where(jnp.eye(row_count, dtype=bool), jnp.float32(0.0), coefficient)
    return jnp.dot(coefficient, partner, precision=lax.Precision.HIGHEST)


def permuted(values, axis, size, mask):
    def branch(value):
        pairs = [(at, at ^ value) for at in range(size)]
        return lambda values: lax.ppermute(values, axis, pairs)

    return lax.switch(mask, [branch(value) for value in range(size)], values)


def by_permutes(features, labels, rounds, across, down):
    blocks = across * down
    mask = jnp.bitwise_xor(jnp.bitwise_xor(rounds[0], rounds[1]), blocks - 1)
    own = lax.axis_index("gx") * down + lax.axis_index("gy")
    near = permuted(permuted(features, "gx", across, mask // down), "gy", down, mask % down)
    pairs = [(at, blocks - 1 - at) for at in range(blocks)]
    flip = lax.ppermute(features, ("gx", "gy"), pairs)
    all_rows = features.shape[0] * blocks
    real_rows = jnp.float32(features.shape[0]) * jnp.sum(labels).astype(jnp.float32)
    fake_rows = jnp.float32(all_rows) - real_rows
    loss_scale = float(all_rows) * float(all_rows) / 16.0

    def weight(other):
        return pair_weight(labels[own], labels[other], real_rows, fake_rows, loss_scale)

    return (
        tile_grad(features, features, weight(own), True)
        + tile_grad(features, near, weight(jnp.bitwise_xor(own, mask)), False)
        + tile_grad(features, flip, weight(blocks - 1 - own), False)
    )


def solution(mesh):
    across, down = mesh.shape["gx"], mesh.shape["gy"]
    blocks = across * down

    def on_device(features, labels, rounds):
        form = by_kernel if blocks <= KERNEL_DEVICES else by_permutes
        return form(features, labels, rounds, across, down)

    return jax.shard_map(
        on_device,
        mesh=mesh,
        in_specs=(P(("gx", "gy"), None), P(), P()),
        out_specs=P(("gx", "gy"), None),
        check_vma=False,
    )
```

```python
import functools

import jax
import jax.numpy as jnp
from jax import lax
from jax.experimental import pallas as pl
from jax.experimental.pallas import tpu as pltpu
from jax.sharding import PartitionSpec as P

MESH = pl.DeviceIdType.MESH
CHUNKS = 8
GROUPS = 2
STEP = 256
SLAB = 32
DIRECT = 1
KERNEL_DEVICES = 64


def pair_weight(label_own, label_other, real_rows, fake_rows, loss_scale):
    both_real = loss_scale / (real_rows * (real_rows - 1.0))
    both_fake = loss_scale / (fake_rows * (fake_rows - 1.0))
    mixed = -loss_scale / (real_rows * fake_rows)
    same = label_own == label_other
    return jnp.where(same, jnp.where(label_own == 1, both_real, both_fake), mixed)


def flipped(index, mask):
    result = index
    bit = 1
    while bit <= mask:
        if mask & bit:
            result = result + bit * (1 - 2 * ((index // bit) % 2))
        bit *= 2
    return result


def split(values):
    high = values.astype(jnp.bfloat16)
    low = (values - high.astype(jnp.float32)).astype(jnp.bfloat16)
    return high, low


def dot_t(left, right):
    return lax.dot_general(
        left, right, (((1,), (1,)), ((), ())), preferred_element_type=jnp.float32
    )


def dot(left, right):
    return jnp.dot(left, right, preferred_element_type=jnp.float32)


def pick_kernel(across, down, rows, width, rounds_ref, labels_ref, pick_ref, weights_ref):
    blocks = across * down
    own = lax.axis_index("gx") * down + lax.axis_index("gy")
    mask = jnp.bitwise_xor(jnp.bitwise_xor(rounds_ref[0], rounds_ref[1]), blocks - 1)
    pick_ref[0] = mask - 1
    label_sum = lax.fori_loop(
        0, blocks, lambda at, total: total + labels_ref[at], jnp.int32(0)
    )
    all_rows = rows * blocks
    real_rows = (label_sum * rows).astype(jnp.float32)
    fake_rows = jnp.float32(all_rows) - real_rows
    loss_scale = float(all_rows) * float(all_rows) / 16.0
    label_own = labels_ref[own]
    others = (label_own, labels_ref[jnp.bitwise_xor(own, mask)], labels_ref[blocks - 1 - own])
    for at, label in enumerate(others):
        weight = pair_weight(label_own, label, real_rows, fake_rows, loss_scale)
        weights_ref[at] = weight * (6.0 / float(width) ** 0.5)


def exchange_kernel(
    mask, across, down, weights_ref, block_ref, grad_ref, held, own_high, own_low, part, both, factor,
    load_sem, send_near, recv_near, send_far, recv_far,
):
    rows, width = block_ref.shape
    blocks = across * down
    chunk = rows // CHUNKS
    group = rows // GROUPS
    per_group = CHUNKS // GROUPS
    own = lax.axis_index("gx") * down + lax.axis_index("gy")
    near = flipped(own, mask)
    far = flipped(own, (blocks - 1) ^ mask)
    flip = flipped(own, blocks - 1)
    direct = DIRECT if 4 * mask < blocks else 0
    peers = (near, far, flip) if direct else (near, far)

    def device(index):
        return (index // down, index % down)

    load = pltpu.make_async_copy(block_ref, held.at[pl.ds(0, rows)], load_sem)
    load.start()

    barrier = pltpu.get_barrier_semaphore()
    for peer in peers:
        pl.semaphore_signal(barrier, inc=1, device_id=device(peer), device_id_type=MESH)
    pl.semaphore_wait(barrier, len(peers))

    def to_near(at):
        return pltpu.make_async_remote_copy(
            src_ref=block_ref.at[pl.ds(at * chunk, chunk)],
            dst_ref=held.at[pl.ds(rows + at * chunk, chunk)],
            send_sem=send_near.at[at],
            recv_sem=recv_near.at[at],
            device_id=device(near),
            device_id_type=MESH,
        )

    def to_far(at):
        return pltpu.make_async_remote_copy(
            src_ref=held.at[pl.ds(rows + at * chunk, chunk)],
            dst_ref=held.at[pl.ds(2 * rows + at * chunk, chunk)],
            send_sem=send_far.at[at],
            recv_sem=recv_far.at[at],
            device_id=device(far),
            device_id_type=MESH,
        )

    def to_flip(at):
        return pltpu.make_async_remote_copy(
            src_ref=block_ref.at[pl.ds(at * chunk, chunk)],
            dst_ref=held.at[pl.ds(2 * rows + at * chunk, chunk)],
            send_sem=send_far.at[at],
            recv_sem=recv_far.at[at],
            device_id=device(flip),
            device_id_type=MESH,
        )

    def each(first, count, body):
        def step(at, carry):
            body(first + at)
            return carry

        lax.fori_loop(0, count, step, 0)

    each(0, CHUNKS, lambda at: to_near(at).start())
    for at in range(direct):
        to_flip(at).start()

    load.wait()

    def prepare(at):
        here = pl.ds(at * SLAB, SLAB)
        high, low = split(held[here, :])
        own_high[here, :] = high
        own_low[here, :] = low
        grad_ref[here, :] = jnp.zeros((SLAB, width), jnp.float32)

    each(0, rows // SLAB, prepare)

    def relay(at):
        to_near(at).wait_recv()

        @pl.when(at >= direct)
        def _():
            to_far(at).start()

    def tile(at):
        which, place = at // GROUPS, at % GROUPS
        each(place * per_group, per_group * (which % 2), relay)
        each(
            place * per_group, per_group * (which // 2), lambda at: to_far(at).wait_recv()
        )

        def split_part(at):
            high, low = split(held[pl.ds(which * rows + place * group + at * SLAB, SLAB), :])
            part[pl.ds(at * SLAB, SLAB), :] = high
            part[pl.ds(group + at * SLAB, SLAB), :] = low

        each(0, group // SLAB, split_part)
        both[...] = jnp.zeros((rows, 2 * group), jnp.float32)

        def depth(at):
            here = pl.ds(pl.multiple_of(at * STEP, STEP), STEP)
            both[...] += dot_t(own_high[:, here], part[:, here])
            both[:, 0:group] += dot_t(own_low[:, here], part[0:group, here])

        each(0, width // STEP, depth)

        def coefficients(at):
            here = pl.ds(at * SLAB, SLAB)
            scores = both[here, 0:group] + both[here, group:]
            raised = scores * (1.0 / float(width) ** 0.5) + 1.0
            coefficient = weights_ref[which] * (raised * raised)
            row = lax.broadcasted_iota(jnp.int32, (SLAB, group), 0) + at * SLAB
            column = lax.broadcasted_iota(jnp.int32, (SLAB, group), 1)
            column = column + (which * rows + place * group)
            coefficient = jnp.where(row == column, 0.0, coefficient)
            high, low = split(coefficient)
            factor[here, 0:group] = high
            factor[here, group : 2 * group] = high
            factor[here, 2 * group :] = low

        each(0, rows // SLAB, coefficients)

        def columns(at):
            here = pl.ds(pl.multiple_of(at * STEP, STEP), STEP)
            grad_ref[:, here] += dot(factor[:, 0 : 2 * group], part[:, here]) + dot(
                factor[:, 2 * group :], part[0:group, here]
            )

        each(0, width // STEP, columns)

    each(0, 3 * GROUPS, tile)

    def finish(at):
        to_near(at).wait_send()
        to_far(at).wait_send()

    each(0, CHUNKS, finish)


def by_kernel(features, labels, rounds, across, down):
    rows, width = features.shape
    blocks = across * down
    smem = pl.BlockSpec(memory_space=pltpu.SMEM)
    pick, weights = pl.pallas_call(
        functools.partial(pick_kernel, across, down, rows, width),
        out_shape=(
            jax.ShapeDtypeStruct((1,), jnp.int32),
            jax.ShapeDtypeStruct((3,), jnp.float32),
        ),
        in_specs=[smem, smem],
        out_specs=(smem, smem),
        compiler_params=pltpu.CompilerParams(vmem_limit_bytes=60 * 1024 * 1024),
        name="mmd_pick",
    )(rounds, labels)

    def branch(value):
        def call(features, weights):
            return pl.pallas_call(
                functools.partial(exchange_kernel, value, across, down),
                out_shape=jax.ShapeDtypeStruct((rows, width), jnp.float32),
                in_specs=[smem, pl.BlockSpec(memory_space=pl.ANY)],
                out_specs=pl.BlockSpec(memory_space=pltpu.VMEM),
                scratch_shapes=[
                    pltpu.VMEM((3 * rows, width), jnp.float32),
                    pltpu.VMEM((rows, width), jnp.bfloat16),
                    pltpu.VMEM((rows, width), jnp.bfloat16),
                    pltpu.VMEM((2 * rows // GROUPS, width), jnp.bfloat16),
                    pltpu.VMEM((rows, 2 * rows // GROUPS), jnp.float32),
                    pltpu.VMEM((rows, 3 * rows // GROUPS), jnp.bfloat16),
                    pltpu.SemaphoreType.DMA,
                    pltpu.SemaphoreType.DMA((CHUNKS,)),
                    pltpu.SemaphoreType.DMA((CHUNKS,)),
                    pltpu.SemaphoreType.DMA((CHUNKS,)),
                    pltpu.SemaphoreType.DMA((CHUNKS,)),
                ],
                compiler_params=pltpu.CompilerParams(
                    collective_id=value,
                    has_side_effects=True,
                    vmem_limit_bytes=32 * 1024 * 1024,
                ),
                cost_estimate=pl.CostEstimate(
                    flops=36 * rows * rows * width,
                    bytes_accessed=12 * rows * width,
                    transcendentals=0,
                ),
                name="mmd_mask_%d" % value,
            )(weights, features)

        return call

    return lax.switch(
        pick[0], [branch(value) for value in range(1, blocks - 1)], features, weights
    )


def tile_grad(own_rows, partner, weight, skip_diag):
    row_count, feat_width = own_rows.shape
    root_width = jnp.sqrt(jnp.float32(feat_width))
    scores = jnp.dot(own_rows, partner.T, precision=lax.Precision.HIGHEST) / root_width
    coefficient = weight * (6.0 / root_width) * (scores + 1.0) ** 2
    if skip_diag:
        coefficient = jnp.where(jnp.eye(row_count, dtype=bool), jnp.float32(0.0), coefficient)
    return jnp.dot(coefficient, partner, precision=lax.Precision.HIGHEST)


def permuted(values, axis, size, mask):
    def branch(value):
        pairs = [(at, at ^ value) for at in range(size)]
        return lambda values: lax.ppermute(values, axis, pairs)

    return lax.switch(mask, [branch(value) for value in range(size)], values)


def by_permutes(features, labels, rounds, across, down):
    blocks = across * down
    mask = jnp.bitwise_xor(jnp.bitwise_xor(rounds[0], rounds[1]), blocks - 1)
    own = lax.axis_index("gx") * down + lax.axis_index("gy")
    near = permuted(permuted(features, "gx", across, mask // down), "gy", down, mask % down)
    pairs = [(at, blocks - 1 - at) for at in range(blocks)]
    flip = lax.ppermute(features, ("gx", "gy"), pairs)
    all_rows = features.shape[0] * blocks
    real_rows = jnp.float32(features.shape[0]) * jnp.sum(labels).astype(jnp.float32)
    fake_rows = jnp.float32(all_rows) - real_rows
    loss_scale = float(all_rows) * float(all_rows) / 16.0

    def weight(other):
        return pair_weight(labels[own], labels[other], real_rows, fake_rows, loss_scale)

    return (
        tile_grad(features, features, weight(own), True)
        + tile_grad(features, near, weight(jnp.bitwise_xor(own, mask)), False)
        + tile_grad(features, flip, weight(blocks - 1 - own), False)
    )


def solution(mesh):
    across, down = mesh.shape["gx"], mesh.shape["gy"]
    blocks = across * down

    def on_device(features, labels, rounds):
        form = by_kernel if blocks <= KERNEL_DEVICES else by_permutes
        return form(features, labels, rounds, across, down)

    return jax.shard_map(
        on_device,
        mesh=mesh,
        in_specs=(P(("gx", "gy"), None), P(), P()),
        out_specs=P(("gx", "gy"), None),
        check_vma=False,
    )
```
